32 devices in a mesh: groups: 2 (over x), expert: 16 (over z, y, core).
Axes of the slice: x: 2, y: 2, z: 4, core: 2. Of those that a mesh axis runs over, the one named last changes fastest.
Arguments:
- resid: bfloat16 [512, 2880], P(('groups', 'expert')), parts along dimension 0, may hold values from -6 to 6
- probe_input: bfloat16 [512, 4096], P(('groups', 'expert')), parts along dimension 0, may hold values from -256 to 256
- key_new: bfloat16 [512, 512], P(('groups', 'expert')), parts along dimension 0, may hold values from -5 to 5
- payload_latest: bfloat16 [512, 512], P(('groups', 'expert')), parts along dimension 0, may hold values from -6 to 6
- cache_keys: bfloat16 [512, 128, 512], P(('groups', 'expert')), parts along dimension 0, may hold values from -5 to 5
- circular_payloads: bfloat16 [512, 128, 512], P(('groups', 'expert')), parts along dimension 0, may hold values from -6 to 6
- cycle_slots: int32 [512], P(('groups', 'expert')), parts along dimension 0, may hold values from 0 to 127
- valid_lengths: int32 [512], P(('groups', 'expert')), parts along dimension 0, may hold values from 2 to 128
- drain_offsets: float32 [64], replicated, may hold values from 0.5 to 4
- w_out: bfloat16 [4096, 2880], P(None, 'expert'), may hold values from -0.09375 to 0.09375
- norm_gain: bfloat16 [2880], replicated, may hold values from 0.099609375 to 1.8984375
- expert_ids: int32 [512, 4], P(('groups', 'expert')), parts along dimension 0, may hold values from 0 to 7, all different within a row; in each aligned block of 16 rows (0 to 15, 16 to 31, ...) at most 12 rows name the same one
- route_codes: int32 [512, 4], P(('groups', 'expert')), parts along dimension 0, may hold values from 16 to 255
- w_gate: bfloat16 [2880, 23040], P(None, 'expert'), may hold values from -0.109375 to 0.109375
- w_up: bfloat16 [2880, 23040], P(None, 'expert'), may hold values from -0.109375 to 0.109375
- w_down: bfloat16 [23040, 2880], P('expert'), may hold values from -0.109375 to 0.109375
Outputs:
- layer_out: bfloat16 [512, 2880], P(('groups', 'expert')), parts along dimension 0
The draws below stay inside these ranges and needn't reach their ends.
There are 2 independent parts, one for each index of `groups`. The reference program is written for one: setup_inputs(seed, part) draws one part's arguments, and reference() takes and returns one part's arrays. A program takes and returns all parts, laid end to end along the dimension named above; an argument that names none is the same for every part. Nothing has to cross between parts.
Inputs may be any that keep to these rules, and one draw needn't show every extreme that they name: `expert_ids`: among the 16 rows of one device (aligned blocks), no expert is named by more than 12 rows; some expert is named by exactly 12 rows in every draw.
All inputs are finite; a program needn't handle non-finite values.
Results may differ from the reference program's by a relative error of at most 0.0055.
Values may be sent and summed in bfloat16 or wider, within the bound.
No kernel may reach another device: no remote copies, remote signals or barrier semaphores. Data moves between devices by JAX's collectives and lax.ppermute only.
A program may use at most 128 MiB of HBM per device.

```python
import math
import jax
import jax.numpy as jnp
import numpy as np
from jax import lax

D = 2880
ASKING_PARTS = 64
SHARED_PAIRS = 8
FEATURE_WIDTH = 64
LOOKBACK_LEN = 128
EXP_FF = 2880
TOPK = 4
EXP_FLIGHT = 8
ROWS_DEV = 16
CAP = 12
LINE_TOTAL = 256
N_EXPERT = 16


def common_draw(key):
    lookup_start = jax.random.truncated_normal(jax.random.fold_in(key, 100), -5.0, 5.0, (LINE_TOTAL, SHARED_PAIRS * FEATURE_WIDTH), jnp.float32)
    chosen = jax.random.randint(jax.random.fold_in(key, 101), (LINE_TOTAL,), 0, LOOKBACK_LEN)
    rowpos = jnp.arange(LINE_TOTAL)
    chosen = jnp.where(rowpos == 1, LOOKBACK_LEN - 1, jnp.where(rowpos == 2, 0, chosen))
    return (lookup_start, chosen.astype(jnp.int32))


def draw_key_new(key, part):
    lookup_start, chosen = common_draw(key)
    return lookup_start.astype(jnp.bfloat16)


def draw_probe_input(key, part):
    key = jax.random.fold_in(key, 2)
    final_mixture = jax.random.truncated_normal(key, -5.0, 5.0, (LINE_TOTAL, ASKING_PARTS * FEATURE_WIDTH), jnp.float32)
    return final_mixture.astype(jnp.bfloat16)


def draw_cache_keys(key, part):
    key = jax.random.fold_in(key, 3)
    final_mixture = jax.random.truncated_normal(key, -5.0, 5.0, (LINE_TOTAL, LOOKBACK_LEN, SHARED_PAIRS * FEATURE_WIDTH), jnp.float32)
    return final_mixture.astype(jnp.bfloat16)


def draw_cycle_slots(key, part):
    lookup_start, chosen = common_draw(key)
    return chosen


def draw_valid_lengths(key, part):
    key = jax.random.fold_in(key, 5)
    drawn = jax.random.randint(key, (LINE_TOTAL,), 2, LOOKBACK_LEN + 1)
    rowpos = jnp.arange(LINE_TOTAL)
    return jnp.where(rowpos == 0, LOOKBACK_LEN, drawn).astype(jnp.int32)


def touch_ends(values, own_key, smallest, largest):
    shape = values.shape
    index_at = [jax.random.randint(jax.random.fold_in(own_key, axis), (), 0, shape[axis]) for axis in range(len(shape))]
    values = values.at[tuple(index_at)].set(smallest)
    longest = shape.index(max(shape))
    index_at[longest] = (index_at[longest] + 1) % shape[longest]
    return values.at[tuple(index_at)].set(largest)


def levels(key, extent, split, low, largest):
    gain = 1.0
    for axis_at, shards_of in split:
        steps = jax.random.uniform(jax.random.fold_in(jax.random.fold_in(key, 6), axis_at), (shards_of,), jnp.float32, low / len(split), largest / len(split))
        gain = gain * jnp.repeat(jnp.exp(steps), extent[axis_at] // shards_of).reshape((-1,) + (1,) * (len(extent) - 1 - axis_at))
    return gain


def deal_out(key, own, number, rows, number_of, top, limit, slope):
    ranking = jax.random.permutation(key, number_of)
    packed, ordinary = shares(number_of, rows * top, limit, slope, True), shares(number_of, rows * top, limit, slope, False)
    places = jnp.arange(number_of)

    def named(tallies, turn):
        used = int((tallies > 0).sum())
        fixed = max(1, used // 4)
        shifted = fixed + (places - fixed + turn * (used - fixed)) % max(1, number_of - fixed)
        return jnp.zeros((number_of,), jnp.int32).at[ranking[jnp.where(places < fixed, places, shifted)]].set(jnp.asarray(tallies, jnp.int32))

    tallies = jnp.where(number % 4 == 0, named(packed, number // 4), named(ordinary, number - number // 4 - 1))
    mixed = jax.random.permutation(jax.random.fold_in(own, 3), number_of)
    donor, receiver = mixed[0:number_of // 2 * 2:2], mixed[1:number_of // 2 * 2:2]
    slack = jnp.minimum(tallies[donor] - 1, limit - tallies[receiver]) // 2
    slack = jnp.where((donor == ranking[0]) | (receiver == ranking[0]) | (tallies[receiver] == 0), 0, jnp.maximum(slack, 0))
    shifted = jax.random.randint(jax.random.fold_in(own, 4), (number_of // 2,), 0, 1 << 20) % (slack + 1)
    tallies = tallies.at[donor].add(-shifted).at[receiver].add(shifted)
    labels = jnp.searchsorted(jnp.cumsum(tallies), jnp.arange(rows * top), side="right").astype(jnp.int32)
    listing = labels.reshape(top, rows).T
    listing = listing[jax.random.permutation(jax.random.fold_in(own, 1), rows)]
    turn = jax.random.randint(jax.random.fold_in(own, 2), (rows, 1), 0, top)
    return jnp.take_along_axis(listing, (jnp.arange(top)[None, :] + turn) % top, axis=1)


def shares(number_of, total, limit, lean, full):
    portions = [(1 << 20) // math.isqrt(standing ** lean) + 1 for standing in range(1, number_of + 1)]
    largest = limit if full else min(limit, max(-(-total // number_of), total * portions[0] // sum(portions)))
    least = 1 if total - largest >= number_of - 1 else 0
    holding, rest = [largest] + [least] * (number_of - 1), total - largest - least * (number_of - 1)
    while rest > 0:
        movable = [i for i in range(1, number_of) if holding[i] < largest] or [i for i in range(1, number_of) if holding[i] < limit]
        whole, budget = sum([portions[i] for i in movable]), rest
        for i in movable:
            more = min(limit - holding[i], max(1, budget * portions[i] // whole), rest)
            holding[i] = holding[i] + more
            rest = rest - more
    return np.array(holding)


def scatter_about(key, shape, spread, most, cuts=(), held_as=jnp.bfloat16):
    result = spread * jax.random.normal(key, shape, jnp.float32)
    if cuts:
        result = result * levels(key, shape, cuts, -0.22, 0.18)
    return jnp.clip(result, -most, most).astype(held_as)


def setup_inputs(seed: int = 0, part: int = 0) -> dict:
    key_list = jax.random.split(jax.random.key(seed), 17)
    part_splits = jax.random.split(jax.random.fold_in(key_list[16], part), 17)
    resid = scatter_about(part_splits[0], (LINE_TOTAL, D), 1.0, 6.0, ((0, 16),))
    probe_input = draw_probe_input(jax.random.fold_in(jax.random.fold_in(key_list[16], part), 71), part)
    key_new = draw_key_new(jax.random.fold_in(jax.random.fold_in(key_list[16], part), 71), part)
    payload_latest = scatter_about(part_splits[3], (LINE_TOTAL, SHARED_PAIRS * FEATURE_WIDTH), 1.0, 6.0, ((0, 16),))
    cache_keys = draw_cache_keys(jax.random.fold_in(jax.random.fold_in(key_list[16], part), 71), part)
    circular_payloads = scatter_about(part_splits[5], (LINE_TOTAL, LOOKBACK_LEN, SHARED_PAIRS * FEATURE_WIDTH), 1.0, 6.0, ((0, 16),))
    cycle_slots = draw_cycle_slots(jax.random.fold_in(jax.random.fold_in(key_list[16], part), 71), part)
    valid_lengths = draw_valid_lengths(jax.random.fold_in(jax.random.fold_in(key_list[16], part), 71), part)
    drain_offsets = jnp.clip(jax.random.uniform(key_list[8], (ASKING_PARTS,), jnp.float32, 0.5, 4.0), 0.5, 4.0)
    w_out = scatter_about(key_list[9], (ASKING_PARTS * FEATURE_WIDTH, D), (ASKING_PARTS * FEATURE_WIDTH) ** -0.5, 0.09375, ((1, 16),))
    norm_gain = jnp.clip(1.0 + 0.18 * jax.random.normal(key_list[10], (D,), jnp.float32), 0.099609375, 1.8984375).astype(jnp.bfloat16)
    expert_ids_keys = jax.random.split(jax.random.fold_in(part_splits[11], 1), LINE_TOTAL // ROWS_DEV)
    expert_ids_turns = jax.random.permutation(jax.random.fold_in(part_splits[11], 3), LINE_TOTAL // ROWS_DEV)
    expert_ids = jax.vmap(lambda own, number: deal_out(jax.random.fold_in(part_splits[11], 2), own, number, ROWS_DEV, EXP_FLIGHT, TOPK, CAP, 1))(expert_ids_keys, expert_ids_turns).reshape((LINE_TOTAL, TOPK))
    route_codes = touch_ends(jax.random.randint(part_splits[12], (LINE_TOTAL, TOPK), 16, 256), jax.random.fold_in(part_splits[12], 1), 16, 255).astype(jnp.int32)
    w_gate = scatter_about(key_list[13], (D, EXP_FLIGHT * EXP_FF), D ** -0.5, 0.109375, ((1, 16),))
    w_up = scatter_about(key_list[14], (D, EXP_FLIGHT * EXP_FF), D ** -0.5, 0.109375, ((1, 16),))
    w_down = scatter_about(key_list[15], (EXP_FLIGHT * EXP_FF, D), EXP_FF ** -0.5, 0.109375, ((0, 16),))
    return dict(resid=resid, probe_input=probe_input, key_new=key_new, payload_latest=payload_latest, cache_keys=cache_keys, circular_payloads=circular_payloads, cycle_slots=cycle_slots, valid_lengths=valid_lengths, drain_offsets=drain_offsets, w_out=w_out, norm_gain=norm_gain, expert_ids=expert_ids, route_codes=route_codes, w_gate=w_gate, w_up=w_up, w_down=w_down)


def attend_rows(probe_input, key_new, payload_latest, cache_keys, circular_payloads, cycle_slots, valid_lengths, drain_offsets):
    line_amount = probe_input.shape[0]
    sharing_ratio = ASKING_PARTS // SHARED_PAIRS
    slot_pos = jnp.arange(LOOKBACK_LEN, dtype=jnp.int32)
    fresh = slot_pos[None, :] == cycle_slots[:, None]
    lookup_entire = jnp.where(fresh[:, :, None], key_new[:, None, :], cache_keys)
    payload_entire = jnp.where(fresh[:, :, None], payload_latest[:, None, :], circular_payloads)
    distance = (cycle_slots[:, None] - slot_pos[None, :]) % LOOKBACK_LEN
    live = distance < valid_lengths[:, None]
    probe_matrix = probe_input.reshape(line_amount, SHARED_PAIRS, sharing_ratio, FEATURE_WIDTH).astype(jnp.float32)
    lookup_widened = lookup_entire.reshape(line_amount, LOOKBACK_LEN, SHARED_PAIRS, FEATURE_WIDTH).astype(jnp.float32)
    payload_widened = payload_entire.reshape(line_amount, LOOKBACK_LEN, SHARED_PAIRS, FEATURE_WIDTH).astype(jnp.float32)
    scores = jnp.einsum('rkgd,rwkd->rkgw', probe_matrix, lookup_widened) / math.sqrt(FEATURE_WIDTH)
    scores = jnp.where(live[:, None, None, :], scores, -jnp.inf)
    drain_bias = drain_offsets.reshape(SHARED_PAIRS, sharing_ratio).astype(jnp.float32)
    top = jnp.maximum(lax.optimization_barrier(jnp.max(scores, axis=-1)), drain_bias[None])
    expo = jnp.exp(scores - top[..., None])
    denom = lax.optimization_barrier(jnp.sum(expo, axis=-1)) + jnp.exp(drain_bias[None] - top)
    probs = expo.astype(jnp.bfloat16).astype(jnp.float32)
    context = jnp.einsum('rkgw,rwkd->rkgd', probs, payload_widened) / denom[..., None]
    return context.reshape(line_amount, ASKING_PARTS * FEATURE_WIDTH).astype(jnp.bfloat16)

def reference(resid, probe_input, key_new, payload_latest, cache_keys, circular_payloads, cycle_slots, valid_lengths, drain_offsets, w_out, norm_gain, expert_ids, route_codes, w_gate, w_up, w_down):
    context = attend_rows(probe_input, key_new, payload_latest, cache_keys, circular_payloads, cycle_slots, valid_lengths, drain_offsets)
    attn = jnp.dot(context, w_out, preferred_element_type=jnp.float32).astype(jnp.bfloat16)
    hstate = resid.astype(jnp.float32) + attn.astype(jnp.float32)
    meansq = lax.optimization_barrier(jnp.mean(hstate * hstate, axis=-1, keepdims=True))
    normed = (hstate * lax.rsqrt(meansq + 1e-05) * norm_gain.astype(jnp.float32)).astype(jnp.bfloat16)
    onehot = (expert_ids[:, :, None] == jnp.arange(EXP_FLIGHT, dtype=jnp.int32)[None, None, :]).astype(jnp.float32)
    codes = route_codes.astype(jnp.float32)
    totals = lax.optimization_barrier(jnp.sum(codes, axis=1))
    gates = (lax.optimization_barrier(jnp.sum(onehot * codes[:, :, None], axis=1)) / totals[:, None]).astype(jnp.bfloat16)
    tensor = N_EXPERT // EXP_FLIGHT
    width = EXP_FF // tensor

    def block_step(accum, block):
        start = (block * width).astype(jnp.int32)
        gate_cols = lax.dynamic_slice_in_dim(w_gate, start, width, 1)
        up_cols = lax.dynamic_slice_in_dim(w_up, start, width, 1)
        down_rows = lax.dynamic_slice_in_dim(w_down, start, width, 0)
        gated = jnp.dot(normed, gate_cols, preferred_element_type=jnp.float32)
        upper = jnp.dot(normed, up_cols, preferred_element_type=jnp.float32)
        act = (gated * jax.nn.sigmoid(1.702 * gated) * (upper + 1.0)).astype(jnp.bfloat16)
        partial_out = jnp.dot(act, down_rows, preferred_element_type=jnp.float32).astype(jnp.bfloat16)
        column = lax.dynamic_slice_in_dim(gates, (block // tensor).astype(jnp.int32), 1, 1).astype(jnp.float32)
        return (accum + column * partial_out.astype(jnp.float32), None)
    combined, _ = lax.scan(block_step, jnp.zeros(hstate.shape, jnp.float32), jnp.arange(N_EXPERT, dtype=jnp.int32))
    return (hstate + combined).astype(jnp.bfloat16)
```

```python
import functools

import jax
import jax.numpy as jnp
from jax import lax
from jax.experimental import pallas as pl
from jax.experimental.pallas import tpu as pltpu
from jax.sharding import PartitionSpec as P

ASKING_PARTS = 64
SHARED_PAIRS = 8
FEATURE_WIDTH = 64
LOOKBACK_LEN = 128
EXP_FF = 2880
EXP_FLIGHT = 8
RATIO = ASKING_PARTS // SHARED_PAIRS
KV = SHARED_PAIRS * FEATURE_WIDTH
LANES = 128
MIB = 1 << 20
BF16 = jnp.bfloat16
F32 = jnp.float32


def attend_kernel(slots, lens, q_ref, kn_ref, vn_ref, k_ref, v_ref, sink_ref, o_ref, qs, os):
    step = pl.program_id(0)
    rows = q_ref.shape[0]
    per_step = k_ref.shape[0]
    half = FEATURE_WIDTH
    low = lax.broadcasted_iota(jnp.int32, (rows, LANES), 1) < half

    @pl.when(step == 0)
    def _():
        for g in range(RATIO):
            for m in range(SHARED_PAIRS // 2):
                t = 8 * m + g // 2
                a = q_ref[:, t * LANES : (t + 1) * LANES].astype(F32)
                b = q_ref[:, (t + 4) * LANES : (t + 5) * LANES].astype(F32)
                if g % 2 == 0:
                    x = jnp.where(low, a, pltpu.roll(b, half, 1))
                else:
                    x = jnp.where(low, pltpu.roll(a, half, 1), b)
                qs[m, pl.ds(g, rows, stride=RATIO), :] = x

    sink = sink_ref[...]
    lane_head = lax.broadcasted_iota(jnp.int32, (RATIO, KV), 1) // FEATURE_WIDTH
    slot_pos = lax.broadcasted_iota(jnp.int32, (LOOKBACK_LEN, KV), 0)
    lane_pos = lax.broadcasted_iota(jnp.int32, (1, LOOKBACK_LEN), 1)
    for r in range(per_step):
        row = step * per_step + r
        slot = slots[row]
        at = pl.multiple_of(row * RATIO, RATIO)
        qrow = jnp.concatenate([qs[m, pl.ds(at, RATIO), :] for m in range(KV // LANES)], axis=1)
        wide = jnp.concatenate(
            [jnp.where(lane_head == h, qrow, 0.0) for h in range(SHARED_PAIRS)], axis=0
        ).astype(BF16)
        fresh = slot_pos == slot
        keys = jnp.where(fresh, kn_ref[r], k_ref[r])
        values = jnp.where(fresh, vn_ref[r], v_ref[r])
        s = lax.dot_general(wide, keys, (((1,), (1,)), ((), ())), preferred_element_type=F32)
        live = ((slot - lane_pos) & (LOOKBACK_LEN - 1)) < lens[row]
        s = jnp.where(live, s * (1.0 / FEATURE_WIDTH**0.5), -1e30)
        top = jnp.maximum(jnp.max(s, axis=1, keepdims=True), sink)
        p = jnp.exp(s - top)
        den = jnp.sum(p, axis=1, keepdims=True) + jnp.exp(sink - top)
        o = jnp.dot(p.astype(BF16), values, preferred_element_type=F32) / den
        ctx = jnp.zeros((RATIO, KV), F32)
        for h in range(SHARED_PAIRS):
            ctx = jnp.where(lane_head == h, o[h * RATIO : (h + 1) * RATIO], ctx)
        for m in range(KV // LANES):
            os[m, pl.ds(at, RATIO), :] = ctx[:, m * LANES : (m + 1) * LANES]

    @pl.when(step == pl.num_programs(0) - 1)
    def _():
        for h in range(SHARED_PAIRS):
            for j in range(RATIO // 2):
                a = os[h // 2, pl.ds(2 * j, rows, stride=RATIO), :]
                b = os[h // 2, pl.ds(2 * j + 1, rows, stride=RATIO), :]
                if h % 2 == 0:
                    x = jnp.where(low, a, pltpu.roll(b, half, 1))
                else:
                    x = jnp.where(low, pltpu.roll(a, half, 1), b)
                t = h * (RATIO // 2) + j
                o_ref[:, t * LANES : (t + 1) * LANES] = x.astype(BF16)


def attend(q, kn, vn, ck, cv, slots, lens, sinks):
    rows = q.shape[0]
    per_step = 4
    whole = lambda shape: pl.BlockSpec(shape, lambda i, *_: (0,) * len(shape))
    split = lambda shape: pl.BlockSpec(shape, lambda i, *_: (i, 0, 0))
    return pl.pallas_call(
        attend_kernel,
        out_shape=jax.ShapeDtypeStruct(q.shape, BF16),
        grid_spec=pltpu.PrefetchScalarGridSpec(
            num_scalar_prefetch=2,
            grid=(rows // per_step,),
            in_specs=[
                whole(q.shape),
                split((per_step, 1, KV)),
                split((per_step, 1, KV)),
                split((per_step, LOOKBACK_LEN, KV)),
                split((per_step, LOOKBACK_LEN, KV)),
                whole((ASKING_PARTS, 1)),
            ],
            out_specs=whole(q.shape),
            scratch_shapes=[pltpu.VMEM((KV // LANES, rows * RATIO, LANES), F32)] * 2,
        ),
        compiler_params=pltpu.CompilerParams(vmem_limit_bytes=16 * MIB),
        name="attend",
    )(slots, lens, q, kn[:, None, :], vn[:, None, :], ck, cv, sinks[:, None])


def hop(x, n, k):
    return lax.ppermute(x, "expert", [(i, i ^ k) for i in range(n)])


def gather(x, n):
    part = {0: x}
    for k in range(4, n, 4):
        part[k] = hop(x, n, k)
    for k in range(0, n, 4):
        part[k + 2] = hop(part[k], n, 2)
    return [part[k] for k in range(0, n, 2)]


def fetch(chip, parts, place, sem):
    copies = [pltpu.make_async_copy(p, place(chip ^ k), sem.at[k]) for k, p in enumerate(parts)]
    for c in copies:
        c.start()
    for c in copies:
        c.wait()


def dot_t(a, b):
    return lax.dot_general(a, b, (((1,), (1,)), ((), ())), preferred_element_type=F32)


def project_kernel(chips, me_ref, *refs):
    parts, (w_ref, wx_ref, res_ref, h_ref, ctx, sem) = refs[:chips], refs[chips:]
    rows = parts[0].shape[0]
    width = w_ref.shape[0]
    me = me_ref[0]
    fetch(me // 2, parts, lambda j: ctx.at[pl.ds(pl.multiple_of(j * rows, rows), rows)], sem)
    mine = dot_t(ctx[...], w_ref[...])
    other = dot_t(ctx[...], wx_ref[...])
    first = me % 2 == 0
    for i in range(2):
        attn = jnp.where(first, mine, other) if i == 0 else jnp.where(first, other, mine)
        res = res_ref[:, i * width : (i + 1) * width].astype(F32)
        h_ref[:, i * width : (i + 1) * width] = (attn.astype(BF16).astype(F32) + res).astype(BF16)
    h_ref[:, 2 * width :] = jnp.zeros((h_ref.shape[0], h_ref.shape[1] - 2 * width), BF16)


def project(me, parts, w_mine, w_other, res):
    chips = len(parts)
    rows, depth = parts[0].shape
    width = -(-2 * w_mine.shape[0] // LANES) * LANES
    return pl.pallas_call(
        functools.partial(project_kernel, chips),
        out_shape=jax.ShapeDtypeStruct((chips * rows, width), BF16),
        in_specs=[pl.BlockSpec(memory_space=pltpu.SMEM)]
        + [pl.BlockSpec(memory_space=pl.ANY)] * chips
        + [pl.BlockSpec(memory_space=pltpu.VMEM)] * 3,
        out_specs=pl.BlockSpec(memory_space=pltpu.VMEM),
        scratch_shapes=[pltpu.VMEM((chips * rows, depth), BF16), pltpu.SemaphoreType.DMA((chips,))],
        compiler_params=pltpu.CompilerParams(vmem_limit_bytes=16 * MIB),
        name="project",
    )(me, *parts, w_mine, w_other, res)


def normalise_kernel(chips, me_ref, *refs):
    parts, (gain, gate, out, own, held, h, sem) = refs[:chips], refs[chips:]
    total, depth = h.shape
    width = depth // chips
    rows = total // chips
    chip = me_ref[0] // 2
    fetch(chip, parts, lambda j: held.at[j], sem)
    for j in range(chips):
        h[:, j * width : (j + 1) * width] = held[j, :, :width]
    own[...] = h[pl.ds(pl.multiple_of(chip * rows, rows), rows), :]
    for i in range(0, total, 32):
        x = h[i : i + 32, :].astype(F32)
        meansq = jnp.sum(x * x, axis=1, keepdims=True) * (1.0 / depth)
        y = x * lax.rsqrt(meansq + 1e-05) * gain[...].astype(F32)
        out[i : i + 32, :depth] = y.astype(BF16)
    out[:, depth:] = jnp.broadcast_to(gate[...], (total, out.shape[1] - depth))


def normalise(me, parts, gain, gate):
    chips = len(parts)
    total, wide = parts[0].shape
    depth = gain.shape[1]
    vmem = pl.BlockSpec(memory_space=pltpu.VMEM)
    padded = -(-(depth + 1) // LANES) * LANES
    return pl.pallas_call(
        functools.partial(normalise_kernel, chips),
        out_shape=[
            jax.ShapeDtypeStruct((total, padded), BF16),
            jax.ShapeDtypeStruct((total // chips, depth), BF16),
        ],
        in_specs=[pl.BlockSpec(memory_space=pltpu.SMEM)]
        + [pl.BlockSpec(memory_space=pl.ANY)] * chips
        + [vmem] * 2,
        out_specs=[vmem] * 2,
        scratch_shapes=[
            pltpu.VMEM((chips, total, wide), BF16),
            pltpu.VMEM((total, depth), BF16),
            pltpu.SemaphoreType.DMA((chips,)),
        ],
        compiler_params=pltpu.CompilerParams(vmem_limit_bytes=16 * MIB),
        name="normalise",
    )(me, *parts, gain, gate)


def expert_kernel(chips, me_ref, x_ref, y_ref, wg, wu, wd, keep, send, h, g_in, u_in, d_in, act, tile, sem):
    half, depth = x_ref.shape[0], wd.shape[1]
    units = act.shape[0]
    rows = half // chips
    chip = me_ref[0] // 2
    block = units // g_in.shape[0]
    copies = {}
    for i in range(g_in.shape[0]):
        part = pl.ds(i * block, block)
        for j, (src, dst) in enumerate(((wg, g_in), (wu, u_in))):
            copies[i, j] = pltpu.make_async_copy(src.at[part], dst.at[i], sem.at[2 * i + j])
    copies[0] = pltpu.make_async_copy(wd, d_in, sem.at[2 * g_in.shape[0]])
    for c in copies.values():
        c.start()
    h[:half] = x_ref[:, :depth]
    h[half:] = y_ref[:, :depth]
    for i in range(g_in.shape[0]):
        copies[i, 0].wait()
        g = dot_t(g_in[i], h[...])
        copies[i, 1].wait()
        u = dot_t(u_in[i], h[...])
        act[i * block : (i + 1) * block] = (g * jax.nn.sigmoid(1.702 * g) * (u + 1.0)).astype(BF16)
    copies[0].wait()
    gate = jnp.concatenate([r[:, depth : depth + 1] for r in (x_ref, y_ref)], axis=0).astype(F32)
    order = [k for bit in (0, 1) for k in range(bit, chips, 2)]
    for at in range(0, depth, 256):
        size = min(256, depth - at)
        p = lax.dot_general(
            act[...], d_in[:, at : at + size], (((0,), (0,)), ((), ())), preferred_element_type=F32
        )
        tile[:, :size] = (p * gate).astype(BF16)
        for i, k in enumerate(order):
            src = pl.multiple_of((chip ^ k) * rows, rows)
            to = (slice(i * rows, (i + 1) * rows), slice(at, at + size))
            keep[to] = tile[pl.ds(src, rows), :size]
            send[to] = tile[pl.ds(half + src, rows), :size]


def experts(me, x, y, w_gate, w_up, w_down, chips):
    half = x.shape[0]
    units, depth = w_down.shape
    blocks = 2 if units % 32 == 0 else 1
    vmem = pl.BlockSpec(memory_space=pltpu.VMEM)
    hbm = pl.BlockSpec(memory_space=pl.ANY)
    return pl.pallas_call(
        functools.partial(expert_kernel, chips),
        out_shape=[jax.ShapeDtypeStruct((half, depth), BF16)] * 2,
        in_specs=[pl.BlockSpec(memory_space=pltpu.SMEM), vmem, vmem, hbm, hbm, hbm],
        out_specs=[vmem] * 2,
        scratch_shapes=[
            pltpu.VMEM((2 * half, depth), BF16),
            pltpu.VMEM((blocks, units // blocks, depth), BF16),
            pltpu.VMEM((blocks, units // blocks, depth), BF16),
            pltpu.VMEM((units, depth), BF16),
            pltpu.VMEM((units, 2 * half), BF16),
            pltpu.VMEM((2 * half, 256), BF16),
            pltpu.SemaphoreType.DMA((2 * blocks + 1,)),
        ],
        compiler_params=pltpu.CompilerParams(vmem_limit_bytes=48 * MIB),
        name="experts",
    )(me, x, y, w_gate, w_up, w_down)


def local(
    n,
    resid,
    probe_input,
    key_new,
    payload_latest,
    cache_keys,
    circular_payloads,
    cycle_slots,
    valid_lengths,
    drain_offsets,
    w_out,
    norm_gain,
    expert_ids,
    route_codes,
    w_gate,
    w_up,
    w_down,
):
    rows, depth = resid.shape
    chips = n // 2
    width = depth // chips
    me = lax.axis_index("expert").astype(jnp.int32).reshape(1)
    onehot = (
        expert_ids[:, :, None] == jnp.arange(EXP_FLIGHT, dtype=jnp.int32)[None, None, :]
    ).astype(F32)
    codes = route_codes.astype(F32)
    gates = (jnp.sum(onehot * codes[:, :, None], axis=1) / jnp.sum(codes, axis=1)[:, None]).astype(BF16)
    spread = jnp.repeat(gates, chips // EXP_FLIGHT, axis=1)
    outgoing = jnp.concatenate(
        [resid.reshape(rows, chips, width).transpose(1, 0, 2), spread.T[:, :, None]], axis=2
    )
    same_core = [list(range(c, n, 2)) for c in range(2)]
    arrived = lax.all_to_all(
        outgoing, "expert", split_axis=0, concat_axis=0, axis_index_groups=same_core, tiled=True
    ).reshape(chips * rows, width + 1)
    w_mine = w_out.T
    w_other = hop(w_mine, n, 1)
    context = attend(
        probe_input,
        key_new,
        payload_latest,
        cache_keys,
        circular_payloads,
        cycle_slots,
        valid_lengths,
        drain_offsets,
    )
    hpart = project(me, gather(context, n), w_mine, w_other, arrived)
    x, own = normalise(me, gather(hpart, n), norm_gain[None], arrived[:, width:])
    keep, send = experts(me, x, hop(x, n, 1), w_gate.T, w_up.T, w_down, chips)
    total = (keep.astype(F32) + hop(send, n, 1).astype(F32)).astype(BF16)
    mid = total.shape[0] // 2
    out = own.astype(F32)
    for k in reversed(range(n // 4)):
        piece = slice(k * rows, (k + 1) * rows)
        z = total[:mid][piece].astype(F32) + hop(total[mid:][piece], n, 2).astype(F32)
        out = out + (hop(z.astype(BF16), n, 4 * k).astype(F32) if k else z)
    return out.astype(BF16)


def solution(mesh):
    row, rep, col = P(("groups", "expert"), None), P(), P(None, "expert")
    row3, row1 = P(("groups", "expert"), None, None), P(("groups", "expert"))
    in_specs = (row, row, row, row, row3, row3, row1, row1, rep, col, rep, row, row, col, col)
    in_specs += (P("expert", None),)
    body = functools.partial(local, mesh.shape["expert"])
    return jax.shard_map(body, mesh=mesh, in_specs=in_specs, out_specs=row, check_vma=False)
```

```python
import functools

import jax
import jax.numpy as jnp
from jax import lax
from jax.experimental import pallas as pl
from jax.experimental.pallas import tpu as pltpu
from jax.sharding import PartitionSpec as P

ASKING_PARTS = 64
SHARED_PAIRS = 8
FEATURE_WIDTH = 64
LOOKBACK_LEN = 128
EXP_FF = 2880
EXP_FLIGHT = 8
RATIO = ASKING_PARTS // SHARED_PAIRS
KV = SHARED_PAIRS * FEATURE_WIDTH
LANES = 128
MIB = 1 << 20
BF16 = jnp.bfloat16
F32 = jnp.float32


def attend_kernel(
    chips, me_ref, slots_in, lens_in, q_in, kn_in, vn_in, k_hbm, v_hbm, sink_in, r_in, ids_in, codes_in, wg, wu,
    *refs,
):
    o_refs, (g_out, u_out, *scratch) = refs[: chips // 2], refs[chips // 2 :]
    slots, lens, q_ref, kn_ref, vn_ref, sink_ref, resid, ids, codes, block, qs, os, kn, vn, k_ref, v_ref, sem, w_sem = scratch
    rows = q_ref.shape[0]
    pairs = (
        (q_in, q_ref), (kn_in, kn_ref), (vn_in, vn_ref), (sink_in, sink_ref), (slots_in, slots), (lens_in, lens),
        (r_in, resid), (ids_in, ids), (codes_in, codes),
    )
    small = [pltpu.make_async_copy(x, y, w_sem.at[2 + i]) for i, (x, y) in enumerate(pairs)]
    for c in small:
        c.start()
    half = FEATURE_WIDTH
    chunk = rows // sem.shape[0]
    copies = []
    for i in range(sem.shape[0]):
        part = pl.ds(i * chunk, chunk)
        pair = ((k_hbm, k_ref), (v_hbm, v_ref))
        copies.append([pltpu.make_async_copy(x.at[part], y.at[part], sem.at[i, j]) for j, (x, y) in enumerate(pair)])
        for c in copies[-1]:
            c.start()
    loads = [pltpu.make_async_copy(wg, g_out, w_sem.at[0]), pltpu.make_async_copy(wu, u_out, w_sem.at[1])]
    for c in loads:
        c.start()
    low = lax.broadcasted_iota(jnp.int32, (rows, LANES), 1) < half
    for c in small:
        c.wait()
    kn[...] = kn_ref[...].astype(F32)
    vn[...] = vn_ref[...].astype(F32)
    shape = (ASKING_PARTS, ASKING_PARTS)
    here = lax.broadcasted_iota(jnp.int32, shape, 0) == lax.broadcasted_iota(jnp.int32, shape, 1)
    sink = jnp.sum(jnp.where(here, sink_ref[...], 0.0), axis=1, keepdims=True)
    for g in range(RATIO):
        for m in range(SHARED_PAIRS // 2):
            t = 8 * m + g // 2
            a = q_ref[:, t * LANES : (t + 1) * LANES].astype(F32)
            b = q_ref[:, (t + 4) * LANES : (t + 5) * LANES].astype(F32)
            if g % 2 == 0:
                x = jnp.where(low, a, pltpu.roll(b, half, 1))
            else:
                x = jnp.where(low, pltpu.roll(a, half, 1), b)
            qs[m, pl.ds(g, rows, stride=RATIO), :] = x * (1.0 / FEATURE_WIDTH**0.5)

    lane_head = lax.broadcasted_iota(jnp.int32, (RATIO, KV), 1) // FEATURE_WIDTH
    slot_pos = lax.broadcasted_iota(jnp.int32, (LOOKBACK_LEN, KV), 0)
    lane_pos = lax.broadcasted_iota(jnp.int32, (1, LOOKBACK_LEN), 1)
    for row in range(rows):
        if row % chunk == 0:
            for c in copies[row // chunk]:
                c.wait()
        slot = slots[row]
        at = slice(row * RATIO, (row + 1) * RATIO)
        qrow = jnp.concatenate([qs[m, at, :] for m in range(KV // LANES)], axis=1)
        wide = jnp.concatenate(
            [jnp.where(lane_head == h, qrow, 0.0) for h in range(SHARED_PAIRS)], axis=0
        ).astype(BF16)
        fresh = slot_pos == slot
        keys = jnp.where(fresh, kn[row : row + 1, :].astype(BF16), k_ref[row])
        values = jnp.where(fresh, vn[row : row + 1, :].astype(BF16), v_ref[row])
        s = lax.dot_general(wide, keys, (((1,), (1,)), ((), ())), preferred_element_type=F32)
        live = ((slot - lane_pos) & (LOOKBACK_LEN - 1)) < lens[row]
        s = jnp.where(live, s, -1e30)
        top = jnp.maximum(jnp.max(s, axis=1, keepdims=True), sink)
        p = jnp.exp(s - top)
        den = jnp.sum(p, axis=1, keepdims=True) + jnp.exp(sink - top)
        o = jnp.dot(p.astype(BF16), values, preferred_element_type=F32)
        o = o * (1.0 / den)
        ctx = jnp.zeros((RATIO, KV), F32)
        for h in range(SHARED_PAIRS):
            ctx = jnp.where(lane_head == h, o[h * RATIO : (h + 1) * RATIO], ctx)
        for m in range(KV // LANES):
            os[m, at, :] = ctx[:, m * LANES : (m + 1) * LANES]

    for h in range(SHARED_PAIRS):
        for j in range(RATIO // 2):
            a = os[h // 2, pl.ds(2 * j, rows, stride=RATIO), :]
            b = os[h // 2, pl.ds(2 * j + 1, rows, stride=RATIO), :]
            if h % 2 == 0:
                x = jnp.where(low, a, pltpu.roll(b, half, 1))
            else:
                x = jnp.where(low, pltpu.roll(a, half, 1), b)
            t = h * (RATIO // 2) + j
            for o_ref in o_refs:
                o_ref[:, t * LANES : (t + 1) * LANES] = x.astype(BF16)
    place_blocks(me_ref[0] // 2, resid, ids, codes, block, o_refs)
    for c in loads:
        c.wait()


def place_blocks(chip, resid, ids, codes, block, outs):
    chips, rows, wide = block.shape
    width = resid.shape[1] // chips
    diagonal = lax.broadcasted_iota(jnp.int32, (rows, rows), 0) == lax.broadcasted_iota(jnp.int32, (rows, rows), 1)
    column = lambda x: jnp.sum(jnp.where(diagonal, x.astype(F32), 0.0), axis=1, keepdims=True)
    named = [column(ids[k : k + 1]) for k in range(ids.shape[0])]
    code = [column(codes[k : k + 1]) for k in range(ids.shape[0])]
    total = sum(code)
    for j in range(chips):
        expert = float(j * EXP_FLIGHT // chips)
        gate = sum(jnp.where(e == expert, c, 0.0) for e, c in zip(named, code)) / total
        k = chip ^ j
        block[k, :, :width] = resid[:, j * width : (j + 1) * width]
        block[k, :, width:] = jnp.broadcast_to(gate, (rows, wide - width)).astype(BF16)
    for k in range(chips):
        start = outs[0].shape[1] - (2 - k % 2) * wide
        outs[k // 2][:, start : start + wide] = block[k]


def in_hbm(x):
    return pltpu.with_memory_space_constraint(x, pltpu.HBM)


def attend(me, q, kn, vn, ck, cv, slots, lens, sinks, resid, ids, codes, wg, wu, chips):
    rows = q.shape[0]
    vmem, hbm = (pl.BlockSpec(memory_space=m) for m in (pltpu.VMEM, pl.ANY))
    wide = -(-(resid.shape[1] // chips + 1) // LANES) * LANES
    return pl.pallas_call(
        functools.partial(attend_kernel, chips),
        out_shape=[jax.ShapeDtypeStruct((rows, q.shape[1] + 2 * wide), BF16)] * (chips // 2)
        + [pltpu.VMEM(x.shape, BF16) for x in (wg, wu)],
        in_specs=[pl.BlockSpec(memory_space=pltpu.SMEM)] + [hbm] * 13,
        out_specs=[vmem] * (chips // 2 + 2),
        scratch_shapes=[pltpu.SMEM(slots.shape, jnp.int32)] * 2
        + [pltpu.VMEM(x.shape, x.dtype) for x in (q, kn, vn, sinks[None], resid, ids.T, codes.T)]
        + [pltpu.VMEM((chips, rows, wide), BF16)]
        + [pltpu.VMEM((KV // LANES, rows * RATIO, LANES), F32)] * 2
        + [pltpu.VMEM((rows, KV), F32)] * 2
        + [pltpu.VMEM(ck.shape, BF16)] * 2
        + [pltpu.SemaphoreType.DMA((4, 2)), pltpu.SemaphoreType.DMA((11,))],
        cost_estimate=pl.CostEstimate(flops=10**9, bytes_accessed=4 * ck.size, transcendentals=0),
        compiler_params=pltpu.CompilerParams(vmem_limit_bytes=12 * MIB),
        name="attend",
    )(me, *map(in_hbm, (slots, lens, q, kn, vn, ck, cv, sinks[None], resid, ids.T, codes.T, wg, wu)))


def hop(x, n, k):
    return lax.ppermute(x, "expert", [(i, i ^ k) for i in range(n)])


def gather(outs, n):
    part = {0: outs[0]}
    for k in range(4, n, 4):
        part[k] = hop(outs[k // 4], n, k)
    for k in range(0, n, 4):
        part[k + 2] = hop(part[k], n, 2)
    return [part[k] for k in range(0, n, 2)]


def fetch(pairs, sem):
    copies = [pltpu.make_async_copy(a, b, sem.at[i]) for i, (a, b) in enumerate(pairs)]
    for c in copies:
        c.start()
    for c in copies:
        c.wait()


def dot_t(a, b):
    return lax.dot_general(a, b, (((1,), (1,)), ((), ())), preferred_element_type=F32)


def project_kernel(chips, me_ref, *refs):
    parts, (w_hbm, wx_ref, wd, h_ref, d_out, ctx, w_ref, res_ref, sem, w_sem) = refs[:chips], refs[chips:]
    rows = parts[0].shape[0]
    width = w_ref.shape[0]
    depth, wide = ctx.shape[1], res_ref.shape[2]
    me = me_ref[0]
    chip = me // 2
    own = pltpu.make_async_copy(w_hbm, w_ref, w_sem.at[0])
    down = pltpu.make_async_copy(wd, d_out, w_sem.at[1])
    own.start()
    pairs = []
    for k, p in enumerate(parts):
        at = pl.ds(pl.multiple_of((chip ^ k) * rows, rows), rows)
        pairs.append((p.at[:, pl.ds(0, depth)], ctx.at[at]))
        pairs.append((p.at[:, pl.ds(depth + k % 2 * wide, wide)], res_ref.at[chip ^ k]))
    fetch(pairs, sem)
    down.start()
    other = dot_t(ctx[...], wx_ref[...])
    own.wait()
    mine = dot_t(ctx[...], w_ref[...])
    first = me % 2 == 0
    for i in range(2):
        attn = jnp.where(first, mine, other) if i == 0 else jnp.where(first, other, mine)
        attn = attn.astype(BF16).astype(F32)
        cols = slice(i * width, (i + 1) * width)
        for j in range(chips):
            at = slice(j * rows, (j + 1) * rows)
            h_ref[at, cols] = (attn[at] + res_ref[j, :, cols].astype(F32)).astype(BF16)
    for j in range(chips):
        h_ref[j * rows : (j + 1) * rows, 2 * width :] = res_ref[j, :, 2 * width :]
    down.wait()


def project(me, parts, w_mine, w_other, w_down):
    chips = len(parts)
    rows, depth = parts[0].shape[0], w_mine.shape[1]
    wide = (parts[0].shape[1] - depth) // 2
    vmem, hbm = (pl.BlockSpec(memory_space=m) for m in (pltpu.VMEM, pl.ANY))
    return pl.pallas_call(
        functools.partial(project_kernel, chips),
        out_shape=[
            jax.ShapeDtypeStruct((chips * rows, wide), BF16),
            pltpu.VMEM(w_down.shape, BF16),
        ],
        in_specs=[pl.BlockSpec(memory_space=pltpu.SMEM)] + [hbm] * (chips + 1) + [vmem, hbm],
        out_specs=[vmem, vmem],
        scratch_shapes=[
            pltpu.VMEM((chips * rows, depth), BF16),
            pltpu.VMEM(w_mine.shape, BF16),
            pltpu.VMEM((chips, rows, wide), BF16),
            pltpu.SemaphoreType.DMA((2 * chips,)),
            pltpu.SemaphoreType.DMA((2,)),
        ],
        compiler_params=pltpu.CompilerParams(vmem_limit_bytes=8 * MIB * chips // 8 + 4 * MIB),
        name="project",
    )(me, *parts, in_hbm(w_mine), w_other, in_hbm(w_down))


def normalise_kernel(chips, me_ref, *refs):
    parts, (gain, out, own, held, h, sem) = refs[:chips], refs[chips:]
    total, depth = h.shape
    width = depth // chips
    rows = total // chips
    chip = me_ref[0] // 2
    fetch([(p, held.at[chip ^ k]) for k, p in enumerate(parts)], sem)
    for j in range(chips):
        h[:, j * width : (j + 1) * width] = held[j, :, :width]
    own[...] = h[pl.ds(pl.multiple_of(chip * rows, rows), rows), :]
    for i in range(0, total, 32):
        x = h[i : i + 32, :].astype(F32)
        meansq = jnp.sum(x * x, axis=1, keepdims=True) * (1.0 / depth)
        y = x * lax.rsqrt(meansq + 1e-05) * gain[...].astype(F32)
        out[i : i + 32, :depth] = y.astype(BF16)
    out[:, depth:] = jnp.broadcast_to(held[chip, :, width : width + 1], (total, out.shape[1] - depth))


def normalise(me, parts, gain):
    chips = len(parts)
    total, wide = parts[0].shape
    depth = gain.shape[1]
    vmem = pl.BlockSpec(memory_space=pltpu.VMEM)
    padded = -(-(depth + 1) // LANES) * LANES
    return pl.pallas_call(
        functools.partial(normalise_kernel, chips),
        out_shape=[
            jax.ShapeDtypeStruct((total, padded), BF16),
            jax.ShapeDtypeStruct((total // chips, depth), BF16),
        ],
        in_specs=[pl.BlockSpec(memory_space=pltpu.SMEM)]
        + [pl.BlockSpec(memory_space=pl.ANY)] * chips
        + [vmem],
        out_specs=[vmem] * 2,
        scratch_shapes=[
            pltpu.VMEM((chips, total, wide), BF16),
            pltpu.VMEM((total, depth), BF16),
            pltpu.SemaphoreType.DMA((chips,)),
        ],
        compiler_params=pltpu.CompilerParams(vmem_limit_bytes=6 * MIB * chips // 8),
        name="normalise",
    )(me, *parts, gain)


def expert_kernel(chips, me_ref, x_ref, y_ref, wg, wu, wd, keep, send, h, act, tile):
    half, depth = x_ref.shape[0], wd.shape[1]
    units = act.shape[0]
    rows = half // chips
    chip = me_ref[0] // 2
    h[:half] = x_ref[:, :depth]
    h[half:] = y_ref[:, :depth]
    block = 240 if units % 240 == 0 else units
    for i in range(0, units, block):
        g = dot_t(wg[i : i + block], h[...])
        u = dot_t(wu[i : i + block], h[...])
        act[i : i + block] = (g * jax.nn.sigmoid(1.702 * g) * (u + 1.0)).astype(BF16)
    gate = jnp.concatenate([r[:, depth : depth + 1] for r in (x_ref, y_ref)], axis=0).astype(F32)
    order = [k for bit in (0, 1) for k in range(bit, chips, 2)]
    a = act[...].T
    for ref in (keep, send):
        ref[:, depth:] = jnp.zeros((half, ref.shape[1] - depth), BF16)
    step = tile.shape[1]
    for at in range(0, depth, step):
        size = min(step, depth - at)
        p = jnp.dot(a, wd[:, at : at + size], preferred_element_type=F32)
        tile[:, :size] = (p * gate).astype(BF16)
        for i, k in enumerate(order):
            src = pl.multiple_of((chip ^ k) * rows, rows)
            to = (slice(i * rows, (i + 1) * rows), slice(at, at + size))
            keep[to] = tile[pl.ds(src, rows), :size]
            send[to] = tile[pl.ds(half + src, rows), :size]


def experts(me, x, y, w_gate, w_up, w_down, chips):
    half = x.shape[0]
    units, depth = w_down.shape
    vmem = pl.BlockSpec(memory_space=pltpu.VMEM)
    return pl.pallas_call(
        functools.partial(expert_kernel, chips),
        out_shape=[jax.ShapeDtypeStruct((half, x.shape[1]), BF16)] * 2,
        in_specs=[pl.BlockSpec(memory_space=pltpu.SMEM)] + [vmem] * 5,
        out_specs=[vmem] * 2,
        scratch_shapes=[
            pltpu.VMEM((2 * half, depth), BF16),
            pltpu.VMEM((units, 2 * half), BF16),
            pltpu.VMEM((2 * half, 512), BF16),
        ],
        compiler_params=pltpu.CompilerParams(vmem_limit_bytes=8 * MIB * chips // 8),
        name="experts",
    )(me, x, y, w_gate, w_up, w_down)


def local(
    n,
    resid,
    probe_input,
    key_new,
    payload_latest,
    cache_keys,
    circular_payloads,
    cycle_slots,
    valid_lengths,
    drain_offsets,
    w_out,
    norm_gain,
    expert_ids,
    route_codes,
    w_gate,
    w_up,
    w_down,
):
    rows, depth = resid.shape
    chips = n // 2
    me = lax.axis_index("expert").astype(jnp.int32).reshape(1)
    w_mine = w_out.T
    w_other = hop(w_mine, n, 1)
    *context, gate_mat, up_mat = attend(
        me,
        probe_input,
        key_new,
        payload_latest,
        cache_keys,
        circular_payloads,
        cycle_slots,
        valid_lengths,
        drain_offsets,
        resid,
        expert_ids,
        route_codes,
        w_gate.T,
        w_up.T,
        chips,
    )
    hpart, down_mat = project(me, gather(context, n), w_mine, w_other, w_down)
    x, own = normalise(me, gather([hpart] * (chips // 2), n), norm_gain[None])
    keep, send = experts(me, x, hop(x, n, 1), gate_mat, up_mat, down_mat, chips)
    total = (keep.astype(F32) + hop(send, n, 1).astype(F32)).astype(BF16)
    pieces = lax.optimization_barrier(tuple(jnp.split(total, chips)))
    mid = chips // 2
    out = 0
    for k in range(mid - 1, -1, -1):
        z = pieces[k].astype(F32) + hop(pieces[mid + k], n, 2).astype(F32)
        out = out + (hop(z.astype(BF16), n, 4 * k).astype(F32) if k else z)
    return (own.astype(F32) + out[:, :depth]).astype(BF16)


def solution(mesh):
    row, rep, col = P(("groups", "expert"), None), P(), P(None, "expert")
    row3, row1 = P(("groups", "expert"), None, None), P(("groups", "expert"))
    in_specs = (row, row, row, row, row3, row3, row1, row1, rep, col, rep, row, row, col, col)
    in_specs += (P("expert", None),)
    body = functools.partial(local, mesh.shape["expert"])
    return jax.shard_map(body, mesh=mesh, in_specs=in_specs, out_specs=row, check_vma=False)
```

```python
import functools

import jax
import jax.numpy as jnp
from jax import lax
from jax.experimental import pallas as pl
from jax.experimental.pallas import tpu as pltpu
from jax.sharding import PartitionSpec as P

ASKING_PARTS = 64
SHARED_PAIRS = 8
FEATURE_WIDTH = 64
LOOKBACK_LEN = 128
EXP_FF = 2880
EXP_FLIGHT = 8
RATIO = ASKING_PARTS // SHARED_PAIRS
KV = SHARED_PAIRS * FEATURE_WIDTH
LANES = 128
MIB = 1 << 20
BF16 = jnp.bfloat16
F32 = jnp.float32


def attend_kernel(
    chips, me_ref, slots_in, lens_in, q_in, kn_in, vn_in, k_hbm, v_hbm, sink_in, r_in, ids_in, codes_in, wg,
    *refs,
):
    o_refs, (g_out, *scratch) = refs[: chips // 2 + 1], refs[chips // 2 + 1 :]
    slots, lens, q_ref, kn_ref, vn_ref, sink_ref, resid, ids, codes, block, qs, os, kn, vn, k_ref, v_ref, sem, w_sem = scratch
    rows = q_ref.shape[0]
    pairs = (
        (q_in, q_ref), (kn_in, kn_ref), (vn_in, vn_ref), (sink_in, sink_ref), (slots_in, slots), (lens_in, lens),
        (r_in, resid), (ids_in, ids), (codes_in, codes),
    )
    small = [pltpu.make_async_copy(x, y, w_sem.at[2 + i]) for i, (x, y) in enumerate(pairs)]
    for c in small:
        c.start()
    half = FEATURE_WIDTH
    chunk = rows // sem.shape[0]
    copies = []
    for i in range(sem.shape[0]):
        part = pl.ds(i * chunk, chunk)
        pair = ((k_hbm, k_ref), (v_hbm, v_ref))
        copies.append([pltpu.make_async_copy(x.at[part], y.at[part], sem.at[i, j]) for j, (x, y) in enumerate(pair)])
        for c in copies[-1]:
            c.start()
    loads = [pltpu.make_async_copy(wg, g_out, w_sem.at[0])]
    for c in loads:
        c.start()
    low = lax.broadcasted_iota(jnp.int32, (rows, LANES), 1) < half
    for c in small:
        c.wait()
    kn[...] = kn_ref[...].astype(F32)
    vn[...] = vn_ref[...].astype(F32)
    shape = (ASKING_PARTS, ASKING_PARTS)
    here = lax.broadcasted_iota(jnp.int32, shape, 0) == lax.broadcasted_iota(jnp.int32, shape, 1)
    sink = jnp.sum(jnp.where(here, sink_ref[...], 0.0), axis=1, keepdims=True)
    for g in range(RATIO):
        for m in range(SHARED_PAIRS // 2):
            t = 8 * m + g // 2
            a = q_ref[:, t * LANES : (t + 1) * LANES].astype(F32)
            b = q_ref[:, (t + 4) * LANES : (t + 5) * LANES].astype(F32)
            if g % 2 == 0:
                x = jnp.where(low, a, pltpu.roll(b, half, 1))
            else:
                x = jnp.where(low, pltpu.roll(a, half, 1), b)
            qs[m, pl.ds(g, rows, stride=RATIO), :] = x * (1.0 / FEATURE_WIDTH**0.5)

    lane_head = lax.broadcasted_iota(jnp.int32, (RATIO, KV), 1) // FEATURE_WIDTH
    tile_pos = lax.broadcasted_iota(jnp.int32, (16, KV), 0)
    lane_pos = lax.broadcasted_iota(jnp.int32, (1, LOOKBACK_LEN), 1)
    sinks = jnp.concatenate([sink] * chunk, axis=0)
    for first in range(0, rows, chunk):
        group = range(first, first + chunk)
        for c in copies[first // chunk]:
            c.wait()
        for row in group:
            slot = slots[row]
            base = pl.multiple_of(slot // 16 * 16, 16)
            fresh = tile_pos == slot - base
            for new, ref in ((kn, k_ref), (vn, v_ref)):
                old = ref[row, pl.ds(base, 16), :]
                ref[row, pl.ds(base, 16), :] = jnp.where(fresh, new[row : row + 1, :].astype(BF16), old)
        scores = []
        for row in group:
            at = slice(row * RATIO, (row + 1) * RATIO)
            qrow = jnp.concatenate([qs[m, at, :] for m in range(KV // LANES)], axis=1)
            wide = jnp.concatenate(
                [jnp.where(lane_head == h, qrow, 0.0) for h in range(SHARED_PAIRS)], axis=0
            ).astype(BF16)
            s = dot_t(wide, k_ref[row])
            live = ((slots[row] - lane_pos) & (LOOKBACK_LEN - 1)) < lens[row]
            scores.append(jnp.where(live, s, -1e30))
        s = jnp.concatenate(scores, axis=0)
        top = jnp.maximum(jnp.max(s, axis=1, keepdims=True), sinks)
        p = jnp.exp(s - top)
        den = jnp.sum(p, axis=1, keepdims=True) + jnp.exp(sinks - top)
        p = (p * (1.0 / den)).astype(BF16)
        for i, row in enumerate(group):
            at = slice(row * RATIO, (row + 1) * RATIO)
            o = jnp.dot(p[i * ASKING_PARTS : (i + 1) * ASKING_PARTS], v_ref[row], preferred_element_type=F32)
            ctx = o[:RATIO]
            for h in range(1, SHARED_PAIRS):
                ctx = jnp.where(lane_head == h, o[h * RATIO : (h + 1) * RATIO], ctx)
            for m in range(KV // LANES):
                os[m, at, :] = ctx[:, m * LANES : (m + 1) * LANES]

    for h in range(SHARED_PAIRS):
        for j in range(RATIO // 2):
            a = os[h // 2, pl.ds(2 * j, rows, stride=RATIO), :]
            b = os[h // 2, pl.ds(2 * j + 1, rows, stride=RATIO), :]
            if h % 2 == 0:
                x = jnp.where(low, a, pltpu.roll(b, half, 1))
            else:
                x = jnp.where(low, pltpu.roll(a, half, 1), b)
            t = h * (RATIO // 2) + j
            for o_ref in o_refs:
                o_ref[:, t * LANES : (t + 1) * LANES] = x.astype(BF16)
    place_blocks(me_ref[0] // 2, resid, ids, codes, block, o_refs)
    for c in loads:
        c.wait()


def place_blocks(chip, resid, ids, codes, block, outs):
    chips, rows, wide = block.shape
    width = resid.shape[1] // chips
    diagonal = lax.broadcasted_iota(jnp.int32, (rows, rows), 0) == lax.broadcasted_iota(jnp.int32, (rows, rows), 1)
    column = lambda x: jnp.sum(jnp.where(diagonal, x.astype(F32), 0.0), axis=1, keepdims=True)
    named = [column(ids[k : k + 1]) for k in range(ids.shape[0])]
    code = [column(codes[k : k + 1]) for k in range(ids.shape[0])]
    total = sum(code)
    for j in range(chips):
        expert = float(j * EXP_FLIGHT // chips)
        gate = sum(jnp.where(e == expert, c, 0.0) for e, c in zip(named, code)) / total
        k = chip ^ j
        block[k, :, :width] = resid[:, j * width : (j + 1) * width]
        block[k, :, width:] = jnp.broadcast_to(gate, (rows, wide - width)).astype(BF16)
    near, far = outs[0].shape[1] - 2 * wide, outs[0].shape[1] - wide
    for k in range(chips):
        outs[k // 2][:, (near, far)[k % 2] : (far, far + wide)[k % 2]] = block[k]
    outs[-1][:, near:far] = block[3]
    outs[-1][:, far:] = block[1]


def in_hbm(x):
    return pltpu.with_memory_space_constraint(x, pltpu.HBM)


def attend(me, q, kn, vn, ck, cv, slots, lens, sinks, resid, ids, codes, wg, chips):
    rows = q.shape[0]
    vmem, hbm = (pl.BlockSpec(memory_space=m) for m in (pltpu.VMEM, pl.ANY))
    wide = -(-(resid.shape[1] // chips + 1) // LANES) * LANES
    return pl.pallas_call(
        functools.partial(attend_kernel, chips),
        out_shape=[jax.ShapeDtypeStruct((rows, q.shape[1] + 2 * wide), BF16)] * (chips // 2 + 1)
        + [pltpu.VMEM(wg.shape, BF16)],
        in_specs=[pl.BlockSpec(memory_space=pltpu.SMEM)] + [hbm] * 12,
        out_specs=[vmem] * (chips // 2 + 2),
        scratch_shapes=[pltpu.SMEM(slots.shape, jnp.int32)] * 2
        + [pltpu.VMEM(x.shape, x.dtype) for x in (q, kn, vn, sinks[None], resid, ids.T, codes.T)]
        + [pltpu.VMEM((chips, rows, wide), BF16)]
        + [pltpu.VMEM((KV // LANES, rows * RATIO, LANES), F32)] * 2
        + [pltpu.VMEM((rows, KV), F32)] * 2
        + [pltpu.VMEM(ck.shape, BF16)] * 2
        + [pltpu.SemaphoreType.DMA((4, 2)), pltpu.SemaphoreType.DMA((11,))],
        cost_estimate=pl.CostEstimate(flops=10**9, bytes_accessed=4 * ck.size, transcendentals=0),
        compiler_params=pltpu.CompilerParams(vmem_limit_bytes=12 * MIB),
        name="attend",
    )(me, *map(in_hbm, (slots, lens, q, kn, vn, ck, cv, sinks[None], resid, ids.T, codes.T, wg)))


def hop(x, n, k):
    return lax.ppermute(x, "expert", [(i, i ^ k) for i in range(n)])


def load_kernel(w_ref, o_ref, sem):
    copy = pltpu.make_async_copy(w_ref, o_ref, sem)
    copy.start()
    copy.wait()


def load(w):
    return pl.pallas_call(
        load_kernel,
        out_shape=pltpu.VMEM(w.shape, w.dtype),
        in_specs=[pl.BlockSpec(memory_space=pl.ANY)],
        out_specs=pl.BlockSpec(memory_space=pltpu.VMEM),
        scratch_shapes=[pltpu.SemaphoreType.DMA],
        cost_estimate=pl.CostEstimate(flops=0, bytes_accessed=2 * w.size, transcendentals=0),
        compiler_params=pltpu.CompilerParams(vmem_limit_bytes=2 * MIB),
        name="load",
    )(in_hbm(w))


def gather(outs, n, beside=tuple):
    part = {0: outs[0]}
    for k in range(4, n, 4):
        part[k] = hop(outs[k // 4], n, k)
    part[2] = hop(outs[-1], n, 2)
    part[6] = hop(part[2], n, 4)
    made = beside()
    if made:
        part[8], *made = lax.optimization_barrier((part[8], *made))
    for k in range(8, n, 4):
        part[k + 2] = hop(part[k], n, 2)
    return [part[k] for k in range(0, n, 2)], made


def fetch(pairs, sem):
    copies = [pltpu.make_async_copy(a, b, sem.at[i]) for i, (a, b) in enumerate(pairs)]
    for c in copies:
        c.start()
    for c in copies:
        c.wait()


def dot_t(a, b):
    return lax.dot_general(a, b, (((1,), (1,)), ((), ())), preferred_element_type=F32)


def project_kernel(chips, me_ref, *refs):
    parts, (w_hbm, wx_ref, *refs) = refs[:chips], refs[chips:]
    h_refs, (ctx, w_ref, res_ref, sem, w_sem) = refs[: chips // 2 + 1], refs[chips // 2 + 1 :]
    h_ref = h_refs[0]
    rows = parts[0].shape[0]
    width = w_ref.shape[0]
    depth, wide = ctx.shape[1], res_ref.shape[2]
    me = me_ref[0]
    chip = me // 2
    own = pltpu.make_async_copy(w_hbm, w_ref, w_sem.at[0])
    own.start()
    pairs = []
    for k, p in enumerate(parts):
        at = pl.ds(pl.multiple_of((chip ^ k) * rows, rows), rows)
        pairs.append((p.at[:, pl.ds(0, depth)], ctx.at[at]))
        far = k % 2 * (k != 3)
        pairs.append((p.at[:, pl.ds(depth + far * wide, wide)], res_ref.at[chip ^ k]))
    fetch(pairs, sem)
    other = dot_t(ctx[...], wx_ref[...])
    own.wait()
    mine = dot_t(ctx[...], w_ref[...])
    first = me % 2 == 0
    for i in range(2):
        attn = jnp.where(first, mine, other) if i == 0 else jnp.where(first, other, mine)
        attn = attn.astype(BF16).astype(F32)
        cols = slice(i * width, (i + 1) * width)
        for j in range(chips):
            at = slice(j * rows, (j + 1) * rows)
            h_ref[at, cols] = (attn[at] + res_ref[j, :, cols].astype(F32)).astype(BF16)
    for j in range(chips):
        h_ref[j * rows : (j + 1) * rows, 2 * width :] = res_ref[j, :, 2 * width :]
    for ref in h_refs[1:]:
        ref[...] = h_ref[...]


def project(me, parts, w_mine, w_other):
    chips = len(parts)
    rows, depth = parts[0].shape[0], w_mine.shape[1]
    wide = (parts[0].shape[1] - depth) // 2
    vmem, hbm = (pl.BlockSpec(memory_space=m) for m in (pltpu.VMEM, pl.ANY))
    return pl.pallas_call(
        functools.partial(project_kernel, chips),
        out_shape=[
            jax.ShapeDtypeStruct((chips * rows, wide), BF16),
        ]
        * (chips // 2 + 1),
        in_specs=[pl.BlockSpec(memory_space=pltpu.SMEM)] + [hbm] * (chips + 1) + [vmem],
        out_specs=[vmem] * (chips // 2 + 1),
        scratch_shapes=[
            pltpu.VMEM((chips * rows, depth), BF16),
            pltpu.VMEM(w_mine.shape, BF16),
            pltpu.VMEM((chips, rows, wide), BF16),
            pltpu.SemaphoreType.DMA((2 * chips,)),
            pltpu.SemaphoreType.DMA((2,)),
        ],
        compiler_params=pltpu.CompilerParams(vmem_limit_bytes=8 * MIB * chips // 8 + 4 * MIB),
        name="project",
    )(me, *parts, in_hbm(w_mine), w_other)


def normalise_kernel(chips, me_ref, *refs):
    parts, (gain, out, own, held, h, sem) = refs[:chips], refs[chips:]
    total, depth = h.shape
    width = depth // chips
    rows = total // chips
    chip = me_ref[0] // 2
    fetch([(p, held.at[chip ^ k]) for k, p in enumerate(parts)], sem)
    for j in range(chips):
        h[:, j * width : (j + 1) * width] = held[j, :, :width]
    own[...] = h[pl.ds(pl.multiple_of(chip * rows, rows), rows), :]
    for i in range(0, total, 32):
        x = h[i : i + 32, :].astype(F32)
        meansq = jnp.sum(x * x, axis=1, keepdims=True) * (1.0 / depth)
        y = x * lax.rsqrt(meansq + 1e-05) * gain[...].astype(F32)
        out[i : i + 32, :depth] = y.astype(BF16)
    out[:, depth:] = jnp.broadcast_to(held[chip, :, width : width + 1], (total, out.shape[1] - depth))


def normalise(me, parts, gain):
    chips = len(parts)
    total, wide = parts[0].shape
    depth = gain.shape[1]
    vmem = pl.BlockSpec(memory_space=pltpu.VMEM)
    padded = -(-(depth + 1) // LANES) * LANES
    return pl.pallas_call(
        functools.partial(normalise_kernel, chips),
        out_shape=[
            jax.ShapeDtypeStruct((total, padded), BF16),
            jax.ShapeDtypeStruct((total // chips, depth), BF16),
        ],
        in_specs=[pl.BlockSpec(memory_space=pltpu.SMEM)]
        + [pl.BlockSpec(memory_space=pl.ANY)] * chips
        + [vmem],
        out_specs=[vmem] * 2,
        scratch_shapes=[
            pltpu.VMEM((chips, total, wide), BF16),
            pltpu.VMEM((total, depth), BF16),
            pltpu.SemaphoreType.DMA((chips,)),
        ],
        compiler_params=pltpu.CompilerParams(vmem_limit_bytes=6 * MIB * chips // 8),
        name="normalise",
    )(me, *parts, gain)


def piece_order(chips):
    return [0, 1, *range(4, chips), 2, 3]


def expert_kernel(chips, me_ref, x_ref, y_ref, wg, wu, wd, keep, send, h, act, tile):
    half, depth = x_ref.shape[0], wd.shape[1]
    units = act.shape[0]
    rows = half // chips
    chip = me_ref[0] // 2
    h[:half] = x_ref[:, :depth]
    h[half:] = y_ref[:, :depth]
    block = 240 if units % 240 == 0 else units
    for i in range(0, units, block):
        g = dot_t(wg[i : i + block], h[...])
        u = dot_t(wu[i : i + block], h[...])
        act[i : i + block] = (g * jax.nn.sigmoid(1.702 * g) * (u + 1.0)).astype(BF16)
    gate = jnp.concatenate([r[:, depth : depth + 1] for r in (x_ref, y_ref)], axis=0).astype(F32)
    order = piece_order(chips)
    a = act[...].T
    for ref in (keep, send):
        ref[:, depth:] = jnp.zeros((half, ref.shape[1] - depth), BF16)
    step = tile.shape[1]
    for at in range(0, depth, step):
        size = min(step, depth - at)
        p = jnp.dot(a, wd[:, at : at + size], preferred_element_type=F32)
        tile[:, :size] = (p * gate).astype(BF16)
        for i, k in enumerate(order):
            src = pl.multiple_of((chip ^ k) * rows, rows)
            to = (slice(i * rows, (i + 1) * rows), slice(at, at + size))
            keep[to] = tile[pl.ds(src, rows), :size]
            send[to] = tile[pl.ds(half + src, rows), :size]


def experts(me, x, y, w_gate, w_up, w_down, chips):
    half = x.shape[0]
    units, depth = w_down.shape
    vmem = pl.BlockSpec(memory_space=pltpu.VMEM)
    return pl.pallas_call(
        functools.partial(expert_kernel, chips),
        out_shape=[jax.ShapeDtypeStruct((half, x.shape[1]), BF16)] * 2,
        in_specs=[pl.BlockSpec(memory_space=pltpu.SMEM)] + [vmem] * 5,
        out_specs=[vmem] * 2,
        scratch_shapes=[
            pltpu.VMEM((2 * half, depth), BF16),
            pltpu.VMEM((units, 2 * half), BF16),
            pltpu.VMEM((2 * half, 512), BF16),
        ],
        compiler_params=pltpu.CompilerParams(vmem_limit_bytes=8 * MIB * chips // 8),
        name="experts",
    )(me, x, y, w_gate, w_up, w_down)


def local(
    n,
    resid,
    probe_input,
    key_new,
    payload_latest,
    cache_keys,
    circular_payloads,
    cycle_slots,
    valid_lengths,
    drain_offsets,
    w_out,
    norm_gain,
    expert_ids,
    route_codes,
    w_gate,
    w_up,
    w_down,
):
    rows, depth = resid.shape
    chips = n // 2
    me = lax.axis_index("expert").astype(jnp.int32).reshape(1)
    w_mine = w_out.T
    w_other = hop(w_mine, n, 1)
    *context, gate_mat = attend(
        me,
        probe_input,
        key_new,
        payload_latest,
        cache_keys,
        circular_payloads,
        cycle_slots,
        valid_lengths,
        drain_offsets,
        resid,
        expert_ids,
        route_codes,
        w_gate.T,
        chips,
    )
    context[0], up, down = lax.optimization_barrier((context[0], w_up.T, w_down))
    parts, (up_mat, down_mat) = gather(context, n, lambda: (load(up), load(down)))
    hpart = project(me, parts, w_mine, w_other)
    x, own = normalise(me, gather(hpart, n)[0], norm_gain[None])
    keep, send = experts(me, x, hop(x, n, 1), gate_mat, up_mat, down_mat, chips)
    total = (keep.astype(F32) + hop(send, n, 1).astype(F32)).astype(BF16)
    order = piece_order(chips)
    cuts = [total[i * rows : (i + 1) * rows] for i in range(chips - 2)]
    *pieces, near = lax.optimization_barrier((*cuts, total[(chips - 2) * rows :]))
    piece = dict(zip(order, pieces))
    add = lambda *xs: sum(x.astype(F32) for x in xs)
    far = {k: hop(piece[k + 1], n, 2) for k in range(chips - 2, 2, -2)}
    near = hop(near, n, 4)
    there = add(piece[1], near[rows:]).astype(BF16)
    out = add(piece[0], near[:rows])
    for k in range(chips - 2, 2, -2):
        out = out + hop(add(piece[k], far[k]).astype(BF16), n, 2 * k).astype(F32)
    out = out + hop(there, n, 2).astype(F32)
    return (own.astype(F32) + out[:, :depth]).astype(BF16)


def solution(mesh):
    row, rep, col = P(("groups", "expert"), None), P(), P(None, "expert")
    row3, row1 = P(("groups", "expert"), None, None), P(("groups", "expert"))
    in_specs = (row, row, row, row, row3, row3, row1, row1, rep, col, rep, row, row, col, col)
    in_specs += (P("expert", None),)
    body = functools.partial(local, mesh.shape["expert"])
    return jax.shard_map(body, mesh=mesh, in_specs=in_specs, out_specs=row, check_vma=False)
```

```python
import functools

import jax
import jax.numpy as jnp
from jax import lax
from jax.experimental import pallas as pl
from jax.experimental.pallas import tpu as pltpu
from jax.sharding import PartitionSpec as P

ASKING_PARTS = 64
SHARED_PAIRS = 8
FEATURE_WIDTH = 64
LOOKBACK_LEN = 128
EXP_FF = 2880
EXP_FLIGHT = 8
RATIO = ASKING_PARTS // SHARED_PAIRS
KV = SHARED_PAIRS * FEATURE_WIDTH
LANES = 128
MIB = 1 << 20
BF16 = jnp.bfloat16
F32 = jnp.float32


def attend_kernel(
    chips, me_ref, slots_in, lens_in, q_in, kn_in, vn_in, k_hbm, v_hbm, sink_in, r_in, ids_in, codes_in, wg,
    *refs,
):
    o_refs, (g_out, *scratch) = refs[: chips // 2 + 1], refs[chips // 2 + 1 :]
    slots, lens, q_ref, kn_ref, vn_ref, sink_ref, resid, ids, codes, block, qs, os, kn, vn, k_ref, v_ref, sem, w_sem = scratch
    rows = q_ref.shape[0]
    pairs = (
        (q_in, q_ref), (kn_in, kn_ref), (vn_in, vn_ref), (sink_in, sink_ref), (slots_in, slots), (lens_in, lens),
        (r_in, resid), (ids_in, ids), (codes_in, codes),
    )
    small = [pltpu.make_async_copy(x, y, w_sem.at[2 + i]) for i, (x, y) in enumerate(pairs)]
    for c in small:
        c.start()
    half = FEATURE_WIDTH
    chunk = rows // sem.shape[0]
    copies = []
    for i in range(sem.shape[0]):
        part = pl.ds(i * chunk, chunk)
        pair = ((k_hbm, k_ref), (v_hbm, v_ref))
        copies.append([pltpu.make_async_copy(x.at[part], y.at[part], sem.at[i, j]) for j, (x, y) in enumerate(pair)])
        for c in copies[-1]:
            c.start()
    loads = [pltpu.make_async_copy(wg, g_out, w_sem.at[0])]
    for c in loads:
        c.start()
    low = lax.broadcasted_iota(jnp.int32, (rows, LANES), 1) < half
    for c in small:
        c.wait()
    kn[...] = kn_ref[...].astype(F32)
    vn[...] = vn_ref[...].astype(F32)
    shape = (ASKING_PARTS, ASKING_PARTS)
    here = lax.broadcasted_iota(jnp.int32, shape, 0) == lax.broadcasted_iota(jnp.int32, shape, 1)
    sink = jnp.sum(jnp.where(here, sink_ref[...], 0.0), axis=1, keepdims=True)
    for g in range(RATIO):
        for m in range(SHARED_PAIRS // 2):
            t = 8 * m + g // 2
            a = q_ref[:, t * LANES : (t + 1) * LANES].astype(F32)
            b = q_ref[:, (t + 4) * LANES : (t + 5) * LANES].astype(F32)
            if g % 2 == 0:
                x = jnp.where(low, a, pltpu.roll(b, half, 1))
            else:
                x = jnp.where(low, pltpu.roll(a, half, 1), b)
            qs[m, pl.ds(g, rows, stride=RATIO), :] = x * (1.0 / FEATURE_WIDTH**0.5)

    lane_head = lax.broadcasted_iota(jnp.int32, (RATIO, KV), 1) // FEATURE_WIDTH
    tile_pos = lax.broadcasted_iota(jnp.int32, (16, KV), 0)
    lane_pos = lax.broadcasted_iota(jnp.int32, (1, LOOKBACK_LEN), 1)
    sinks = jnp.concatenate([sink] * chunk, axis=0)
    for first in range(0, rows, chunk):
        group = range(first, first + chunk)
        for c in copies[first // chunk]:
            c.wait()
        for row in group:
            slot = slots[row]
            base = pl.multiple_of(slot // 16 * 16, 16)
            fresh = tile_pos == slot - base
            for new, ref in ((kn, k_ref), (vn, v_ref)):
                old = ref[row, pl.ds(base, 16), :]
                ref[row, pl.ds(base, 16), :] = jnp.where(fresh, new[row : row + 1, :].astype(BF16), old)
        scores = []
        for row in group:
            at = slice(row * RATIO, (row + 1) * RATIO)
            qrow = jnp.concatenate([qs[m, at, :] for m in range(KV // LANES)], axis=1)
            wide = jnp.concatenate(
                [jnp.where(lane_head == h, qrow, 0.0) for h in range(SHARED_PAIRS)], axis=0
            ).astype(BF16)
            s = dot_t(wide, k_ref[row])
            live = ((slots[row] - lane_pos) & (LOOKBACK_LEN - 1)) < lens[row]
            scores.append(jnp.where(live, s, -1e30))
        s = jnp.concatenate(scores, axis=0)
        top = jnp.maximum(jnp.max(s, axis=1, keepdims=True), sinks)
        p = jnp.exp(s - top)
        den = jnp.sum(p, axis=1, keepdims=True) + jnp.exp(sinks - top)
        p = (p * (1.0 / den)).astype(BF16)
        for i, row in enumerate(group):
            at = slice(row * RATIO, (row + 1) * RATIO)
            o = jnp.dot(p[i * ASKING_PARTS : (i + 1) * ASKING_PARTS], v_ref[row], preferred_element_type=F32)
            ctx = o[:RATIO]
            for h in range(1, SHARED_PAIRS):
                ctx = jnp.where(lane_head == h, o[h * RATIO : (h + 1) * RATIO], ctx)
            for m in range(KV // LANES):
                os[m, at, :] = ctx[:, m * LANES : (m + 1) * LANES]

    for h in range(SHARED_PAIRS):
        for j in range(RATIO // 2):
            a = os[h // 2, pl.ds(2 * j, rows, stride=RATIO), :]
            b = os[h // 2, pl.ds(2 * j + 1, rows, stride=RATIO), :]
            if h % 2 == 0:
                x = jnp.where(low, a, pltpu.roll(b, half, 1))
            else:
                x = jnp.where(low, pltpu.roll(a, half, 1), b)
            t = h * (RATIO // 2) + j
            for o_ref in o_refs:
                o_ref[:, t * LANES : (t + 1) * LANES] = x.astype(BF16)
    place_blocks(me_ref[0] // 2, resid, ids, codes, block, o_refs)
    for c in loads:
        c.wait()


def place_blocks(chip, resid, ids, codes, block, outs):
    chips, rows, wide = block.shape
    width = resid.shape[1] // chips
    diagonal = lax.broadcasted_iota(jnp.int32, (rows, rows), 0) == lax.broadcasted_iota(jnp.int32, (rows, rows), 1)
    column = lambda x: jnp.sum(jnp.where(diagonal, x.astype(F32), 0.0), axis=1, keepdims=True)
    named = [column(ids[k : k + 1]) for k in range(ids.shape[0])]
    code = [column(codes[k : k + 1]) for k in range(ids.shape[0])]
    total = sum(code)
    for j in range(chips):
        expert = float(j * EXP_FLIGHT // chips)
        gate = sum(jnp.where(e == expert, c, 0.0) for e, c in zip(named, code)) / total
        k = chip ^ j
        block[k, :, :width] = resid[:, j * width : (j + 1) * width]
        block[k, :, width:] = jnp.broadcast_to(gate, (rows, wide - width)).astype(BF16)
    near, far = outs[0].shape[1] - 2 * wide, outs[0].shape[1] - wide
    for k in range(chips):
        outs[k // 2][:, (near, far)[k % 2] : (far, far + wide)[k % 2]] = block[k]
    outs[-1][:, near:far] = block[3]
    outs[-1][:, far:] = block[1]


def in_hbm(x):
    return pltpu.with_memory_space_constraint(x, pltpu.HBM)


def attend(me, q, kn, vn, ck, cv, slots, lens, sinks, resid, ids, codes, wg, chips):
    rows = q.shape[0]
    vmem, hbm = (pl.BlockSpec(memory_space=m) for m in (pltpu.VMEM, pl.ANY))
    wide = -(-(resid.shape[1] // chips + 1) // LANES) * LANES
    return pl.pallas_call(
        functools.partial(attend_kernel, chips),
        out_shape=[jax.ShapeDtypeStruct((rows, q.shape[1] + 2 * wide), BF16)] * (chips // 2 + 1)
        + [pltpu.VMEM(wg.shape, BF16)],
        in_specs=[pl.BlockSpec(memory_space=pltpu.SMEM)] + [hbm] * 12,
        out_specs=[vmem] * (chips // 2 + 2),
        scratch_shapes=[pltpu.SMEM(slots.shape, jnp.int32)] * 2
        + [pltpu.VMEM(x.shape, x.dtype) for x in (q, kn, vn, sinks[None], resid, ids.T, codes.T)]
        + [pltpu.VMEM((chips, rows, wide), BF16)]
        + [pltpu.VMEM((KV // LANES, rows * RATIO, LANES), F32)] * 2
        + [pltpu.VMEM((rows, KV), F32)] * 2
        + [pltpu.VMEM(ck.shape, BF16)] * 2
        + [pltpu.SemaphoreType.DMA((2, 2)), pltpu.SemaphoreType.DMA((11,))],
        cost_estimate=pl.CostEstimate(flops=10**9, bytes_accessed=4 * ck.size, transcendentals=0),
        compiler_params=pltpu.CompilerParams(vmem_limit_bytes=12 * MIB),
        name="attend",
    )(me, *map(in_hbm, (slots, lens, q, kn, vn, ck, cv, sinks[None], resid, ids.T, codes.T, wg)))


def hop(x, n, k):
    return lax.ppermute(x, "expert", [(i, i ^ k) for i in range(n)])


def load_kernel(w_ref, o_ref, sem):
    copy = pltpu.make_async_copy(w_ref, o_ref, sem)
    copy.start()
    copy.wait()


def load(w):
    return pl.pallas_call(
        load_kernel,
        out_shape=pltpu.VMEM(w.shape, w.dtype),
        in_specs=[pl.BlockSpec(memory_space=pl.ANY)],
        out_specs=pl.BlockSpec(memory_space=pltpu.VMEM),
        scratch_shapes=[pltpu.SemaphoreType.DMA],
        cost_estimate=pl.CostEstimate(flops=0, bytes_accessed=2 * w.size, transcendentals=0),
        compiler_params=pltpu.CompilerParams(vmem_limit_bytes=2 * MIB),
        name="load",
    )(in_hbm(w))


def gather(outs, n, beside=tuple):
    part = {0: outs[0]}
    for k in range(4, n, 4):
        part[k] = hop(outs[k // 4], n, k)
    part[2] = hop(outs[-1], n, 2)
    part[6] = hop(part[2], n, 4)
    made = beside()
    if made:
        part[8], *made = lax.optimization_barrier((part[8], *made))
    for k in range(8, n, 4):
        part[k + 2] = hop(part[k], n, 2)
    return [part[k] for k in range(0, n, 2)], made


def fetch(pairs, sem):
    copies = [pltpu.make_async_copy(a, b, sem.at[i]) for i, (a, b) in enumerate(pairs)]
    for c in copies:
        c.start()
    for c in copies:
        c.wait()


def dot_t(a, b):
    return lax.dot_general(a, b, (((1,), (1,)), ((), ())), preferred_element_type=F32)


def project_kernel(chips, me_ref, *refs):
    parts, (w_hbm, wx_ref, *refs) = refs[:chips], refs[chips:]
    h_refs, (ctx, w_ref, res_ref, sem, w_sem) = refs[: chips // 2 + 1], refs[chips // 2 + 1 :]
    h_ref = h_refs[0]
    rows = parts[0].shape[0]
    width = w_ref.shape[0]
    depth, wide = ctx.shape[1], res_ref.shape[2]
    me = me_ref[0]
    chip = me // 2
    own = pltpu.make_async_copy(w_hbm, w_ref, w_sem.at[0])
    own.start()
    pairs = []
    for k, p in enumerate(parts):
        at = pl.ds(pl.multiple_of((chip ^ k) * rows, rows), rows)
        pairs.append((p.at[:, pl.ds(0, depth)], ctx.at[at]))
        far = k % 2 * (k != 3)
        pairs.append((p.at[:, pl.ds(depth + far * wide, wide)], res_ref.at[chip ^ k]))
    fetch(pairs, sem)
    other = dot_t(ctx[...], wx_ref[...])
    own.wait()
    mine = dot_t(ctx[...], w_ref[...])
    first = me % 2 == 0
    for i in range(2):
        attn = jnp.where(first, mine, other) if i == 0 else jnp.where(first, other, mine)
        attn = attn.astype(BF16).astype(F32)
        cols = slice(i * width, (i + 1) * width)
        for j in range(chips):
            at = slice(j * rows, (j + 1) * rows)
            h_ref[at, cols] = (attn[at] + res_ref[j, :, cols].astype(F32)).astype(BF16)
    for j in range(chips):
        h_ref[j * rows : (j + 1) * rows, 2 * width :] = res_ref[j, :, 2 * width :]
    for ref in h_refs[1:]:
        ref[...] = h_ref[...]


def project(me, parts, w_mine, w_other):
    chips = len(parts)
    rows, depth = parts[0].shape[0], w_mine.shape[1]
    wide = (parts[0].shape[1] - depth) // 2
    vmem, hbm = (pl.BlockSpec(memory_space=m) for m in (pltpu.VMEM, pl.ANY))
    return pl.pallas_call(
        functools.partial(project_kernel, chips),
        out_shape=[
            jax.ShapeDtypeStruct((chips * rows, wide), BF16),
        ]
        * (chips // 2 + 1),
        in_specs=[pl.BlockSpec(memory_space=pltpu.SMEM)] + [hbm] * (chips + 1) + [vmem],
        out_specs=[vmem] * (chips // 2 + 1),
        scratch_shapes=[
            pltpu.VMEM((chips * rows, depth), BF16),
            pltpu.VMEM(w_mine.shape, BF16),
            pltpu.VMEM((chips, rows, wide), BF16),
            pltpu.SemaphoreType.DMA((2 * chips,)),
            pltpu.SemaphoreType.DMA((2,)),
        ],
        compiler_params=pltpu.CompilerParams(vmem_limit_bytes=8 * MIB * chips // 8 + 4 * MIB),
        name="project",
    )(me, *parts, in_hbm(w_mine), w_other)


def normalise_kernel(chips, me_ref, *refs):
    parts, (gain, out, own, held, h, sem) = refs[:chips], refs[chips:]
    total, depth = h.shape
    width = depth // chips
    rows = total // chips
    chip = me_ref[0] // 2
    fetch([(p, held.at[chip ^ k]) for k, p in enumerate(parts)], sem)
    for j in range(chips):
        h[:, j * width : (j + 1) * width] = held[j, :, :width]
    own[...] = h[pl.ds(pl.multiple_of(chip * rows, rows), rows), :]
    for i in range(0, total, 32):
        x = h[i : i + 32, :].astype(F32)
        meansq = jnp.sum(x * x, axis=1, keepdims=True) * (1.0 / depth)
        y = x * lax.rsqrt(meansq + 1e-05) * gain[...].astype(F32)
        out[i : i + 32, :depth] = y.astype(BF16)
    out[:, depth:] = jnp.broadcast_to(held[chip, :, width : width + 1], (total, out.shape[1] - depth))


def normalise(me, parts, gain):
    chips = len(parts)
    total, wide = parts[0].shape
    depth = gain.shape[1]
    vmem = pl.BlockSpec(memory_space=pltpu.VMEM)
    padded = -(-(depth + 1) // LANES) * LANES
    return pl.pallas_call(
        functools.partial(normalise_kernel, chips),
        out_shape=[
            jax.ShapeDtypeStruct((total, padded), BF16),
            jax.ShapeDtypeStruct((total // chips, depth), BF16),
        ],
        in_specs=[pl.BlockSpec(memory_space=pltpu.SMEM)]
        + [pl.BlockSpec(memory_space=pl.ANY)] * chips
        + [vmem],
        out_specs=[vmem] * 2,
        scratch_shapes=[
            pltpu.VMEM((chips, total, wide), BF16),
            pltpu.VMEM((total, depth), BF16),
            pltpu.SemaphoreType.DMA((chips,)),
        ],
        compiler_params=pltpu.CompilerParams(vmem_limit_bytes=6 * MIB * chips // 8),
        name="normalise",
    )(me, *parts, gain)


def piece_order(chips):
    return [0, 1, *range(4, chips), 2, 3]


def expert_kernel(chips, me_ref, x_ref, y_ref, wg, wu, wd, keep, send, h, act, tile):
    half, depth = x_ref.shape[0], wd.shape[1]
    units = act.shape[0]
    rows = half // chips
    chip = me_ref[0] // 2
    h[:half] = x_ref[:, :depth]
    h[half:] = y_ref[:, :depth]
    block = 240 if units % 240 == 0 else units
    for i in range(0, units, block):
        g = dot_t(wg[i : i + block], h[...])
        u = dot_t(wu[i : i + block], h[...])
        act[i : i + block] = (g * jax.nn.sigmoid(1.702 * g) * (u + 1.0)).astype(BF16)
    gate = jnp.concatenate([r[:, depth : depth + 1] for r in (x_ref, y_ref)], axis=0).astype(F32)
    order = piece_order(chips)
    a = act[...].T
    for ref in (keep, send):
        ref[:, depth:] = jnp.zeros((half, ref.shape[1] - depth), BF16)
    step = tile.shape[1]
    for at in range(0, depth, step):
        size = min(step, depth - at)
        p = jnp.dot(a, wd[:, at : at + size], preferred_element_type=F32)
        tile[:, :size] = (p * gate).astype(BF16)
        for i, k in enumerate(order):
            src = pl.multiple_of((chip ^ k) * rows, rows)
            to = (slice(i * rows, (i + 1) * rows), slice(at, at + size))
            keep[to] = tile[pl.ds(src, rows), :size]
            send[to] = tile[pl.ds(half + src, rows), :size]


def experts(me, x, y, w_gate, w_up, w_down, chips):
    half = x.shape[0]
    units, depth = w_down.shape
    vmem = pl.BlockSpec(memory_space=pltpu.VMEM)
    return pl.pallas_call(
        functools.partial(expert_kernel, chips),
        out_shape=[jax.ShapeDtypeStruct((half, x.shape[1]), BF16)] * 2,
        in_specs=[pl.BlockSpec(memory_space=pltpu.SMEM)] + [vmem] * 5,
        out_specs=[vmem] * 2,
        scratch_shapes=[
            pltpu.VMEM((2 * half, depth), BF16),
            pltpu.VMEM((units, 2 * half), BF16),
            pltpu.VMEM((2 * half, 512), BF16),
        ],
        compiler_params=pltpu.CompilerParams(vmem_limit_bytes=8 * MIB * chips // 8),
        name="experts",
    )(me, x, y, w_gate, w_up, w_down)


def local(
    n,
    resid,
    probe_input,
    key_new,
    payload_latest,
    cache_keys,
    circular_payloads,
    cycle_slots,
    valid_lengths,
    drain_offsets,
    w_out,
    norm_gain,
    expert_ids,
    route_codes,
    w_gate,
    w_up,
    w_down,
):
    rows, depth = resid.shape
    chips = n // 2
    me = lax.axis_index("expert").astype(jnp.int32).reshape(1)
    w_mine = w_out.T
    w_other = hop(w_mine, n, 1)
    *context, gate_mat = attend(
        me,
        probe_input,
        key_new,
        payload_latest,
        cache_keys,
        circular_payloads,
        cycle_slots,
        valid_lengths,
        drain_offsets,
        resid,
        expert_ids,
        route_codes,
        w_gate.T,
        chips,
    )
    context[0], up, down = lax.optimization_barrier((context[0], w_up.T, w_down))
    parts, (up_mat, down_mat) = gather(context, n, lambda: (load(up), load(down)))
    hpart = project(me, parts, w_mine, w_other)
    x, own = normalise(me, gather(hpart, n)[0], norm_gain[None])
    keep, send = experts(me, x, hop(x, n, 1), gate_mat, up_mat, down_mat, chips)
    total = (keep.astype(F32) + hop(send, n, 1).astype(F32)).astype(BF16)
    order = piece_order(chips)
    cuts = [total[i * rows : (i + 1) * rows] for i in range(chips - 2)]
    *pieces, near = lax.optimization_barrier((*cuts, total[(chips - 2) * rows :]))
    piece = dict(zip(order, pieces))
    add = lambda *xs: sum(x.astype(F32) for x in xs)
    far = {k: hop(piece[k + 1], n, 2) for k in range(chips - 2, 2, -2)}
    near = hop(near, n, 4)
    there = add(piece[1], near[rows:]).astype(BF16)
    out = add(piece[0], near[:rows])
    for k in range(chips - 2, 2, -2):
        out = out + hop(add(piece[k], far[k]).astype(BF16), n, 2 * k).astype(F32)
    out = out + hop(there, n, 2).astype(F32)
    return (own.astype(F32) + out[:, :depth]).astype(BF16)


def solution(mesh):
    row, rep, col = P(("groups", "expert"), None), P(), P(None, "expert")
    row3, row1 = P(("groups", "expert"), None, None), P(("groups", "expert"))
    in_specs = (row, row, row, row, row3, row3, row1, row1, rep, col, rep, row, row, col, col)
    in_specs += (P("expert", None),)
    body = functools.partial(local, mesh.shape["expert"])
    return jax.shard_map(body, mesh=mesh, in_specs=in_specs, out_specs=row, check_vma=False)
```
